512 devices in a mesh: pipe: 8 (over y, core), expert: 64 (over z, x).
Axes of the slice: x: 4, y: 4, z: 16, core: 2. Of those that a mesh axis runs over, the one named last changes fastest.
Arguments:
- state: bfloat16 [8, 2, 64, 16, 896], P('pipe', None, 'expert'), may hold values from -6 to 6
- up_weight: bfloat16 [8, 64, 896, 1024], P('pipe', 'expert'), may hold values from -0.0625 to 0.0625
- down_weight: bfloat16 [8, 64, 1024, 896], P('pipe', 'expert'), may hold values from -0.1875 to 0.1875
- norm_gain: float32 [8, 7168], P('pipe'), may hold values from 0.1 to 1.9
- routes: int32 [2, 2, 8, 128, 2], P(None, None, 'pipe'), may hold values from 0 to 7, all different within a row; in each aligned block of 16 rows (0 to 15, 16 to 31, ..., all dimensions but the last counted through in order) at most 8 rows name the same one
- route_weight: float32 [2, 2, 8, 128, 2], P(None, None, 'pipe'), may hold values from 0.1 to 1
Outputs:
- final_state: bfloat16 [8, 2, 64, 16, 896], P('pipe', None, 'expert')
The draws below stay inside these ranges and needn't reach their ends.
Inputs may be any that keep to these rules, and one draw needn't show every extreme that they name: `routes`: each token names 2 different experts; among the 16 tokens of one group at one step, stream and section no expert is named by more than 8 tokens.
All inputs are finite; a program needn't handle non-finite values.
Results may differ from the reference program's by a relative error of at most 0.0059.
Values may be sent and summed in bfloat16 or wider, within the bound.
No kernel may reach another device: no remote copies, remote signals or barrier semaphores. Data moves between devices by JAX's collectives and lax.ppermute only.
A program may use at most 64 MiB of HBM per device.

```python
import math
import jax
import jax.numpy as jnp
import numpy as np
from jax import lax

D = 7168
FFW = 1024
SLICES = 8
TOPK = 2
STEPS = 2
TOK_GRP = 16
DS = 896
GROUPS = 8
CAP = 8
TOKENS = 128
N_PIPE = 8
N_EXPERT = 64


def steps_of(own_key, shape, cuts, low, largest):
    level = 1.0
    for position, shards_of in cuts:
        draws = jax.random.uniform(jax.random.fold_in(jax.random.fold_in(own_key, 6), position), (shards_of,), jnp.float32, low / len(cuts), largest / len(cuts))
        level = level * jnp.repeat(jnp.exp(draws), shape[position] // shards_of).reshape((-1,) + (1,) * (len(shape) - 1 - position))
    return level


def shared_out(rng, own, number, rows, count, top, most, lean):
    order = jax.random.permutation(rng, count)
    heavy_load, ordinary = load_shares(count, rows * top, most, lean, True), load_shares(count, rows * top, most, lean, False)
    places = jnp.arange(count)

    def named(lengths, offset_by):
        used = int((lengths > 0).sum())
        fixed = max(1, used // 4)
        shifted = fixed + (places - fixed + offset_by * (used - fixed)) % max(1, count - fixed)
        return jnp.zeros((count,), jnp.int32).at[order[jnp.where(places < fixed, places, shifted)]].set(jnp.asarray(lengths, jnp.int32))

    lengths = jnp.where(number % 4 == 0, named(heavy_load, number // 4), named(ordinary, number - number // 4 - 1))
    mixed = jax.random.permutation(jax.random.fold_in(own, 3), count)
    giver, sink = mixed[0:count // 2 * 2:2], mixed[1:count // 2 * 2:2]
    room = jnp.minimum(lengths[giver] - 1, most - lengths[sink]) // 2
    room = jnp.where((giver == order[0]) | (sink == order[0]) | (lengths[sink] == 0), 0, jnp.maximum(room, 0))
    shifted = jax.random.randint(jax.random.fold_in(own, 4), (count // 2,), 0, 1 << 20) % (room + 1)
    lengths = lengths.at[giver].add(-shifted).at[sink].add(shifted)
    labels = jnp.searchsorted(jnp.cumsum(lengths), jnp.arange(rows * top), side="right").astype(jnp.int32)
    listing = labels.reshape(top, rows).T
    listing = listing[jax.random.permutation(jax.random.fold_in(own, 1), rows)]
    offset_by = jax.random.randint(jax.random.fold_in(own, 2), (rows, 1), 0, top)
    return jnp.take_along_axis(listing, (jnp.arange(top)[None, :] + offset_by) % top, axis=1)


def load_shares(count, total, limit, skew, full):
    weights = [(1 << 20) // math.isqrt(standing ** skew) + 1 for standing in range(1, count + 1)]
    largest = limit if full else min(limit, max(-(-total // count), total * weights[0] // sum(weights)))
    least = 1 if total - largest >= count - 1 else 0
    holding, spare = [largest] + [least] * (count - 1), total - largest - least * (count - 1)
    while spare > 0:
        candidates = [i for i in range(1, count) if holding[i] < largest] or [i for i in range(1, count) if holding[i] < limit]
        mass, left = sum([weights[i] for i in candidates]), spare
        for i in candidates:
            addition = min(limit - holding[i], max(1, left * weights[i] // mass), spare)
            holding[i] = holding[i] + addition
            spare = spare - addition
    return np.array(holding)


def scatter_about(own_key, extent, spread, most, cuts=(), held_as=jnp.bfloat16):
    values = jax.random.normal(own_key, extent, jnp.float32) * spread
    if len(cuts) > 0:
        values = steps_of(own_key, extent, cuts, -0.22, 0.18) * values
    return jnp.clip(values, min=-most, max=most).astype(held_as)


def setup_inputs(seed: int = 0) -> dict:
    keys = jax.random.split(jax.random.key(seed), 7)
    state = scatter_about(keys[0], (N_PIPE, 2, N_EXPERT, TOK_GRP, DS), 1.0, 6.0, ((0, 8), (2, 64)))
    up_weight = scatter_about(keys[1], (N_PIPE, N_EXPERT, DS, FFW), D ** -0.5, 0.0625, ((0, 8), (1, 64)))
    down_weight = scatter_about(keys[2], (N_PIPE, N_EXPERT, FFW, DS), FFW ** -0.5, 0.1875, ((0, 8), (1, 64)))
    norm_gain = jnp.clip(1.0 + 0.18 * jax.random.normal(keys[3], (N_PIPE, D), jnp.float32), 0.1, 1.9)
    routes_keys = jax.random.split(jax.random.fold_in(keys[4], 1), STEPS * 2 * N_PIPE * TOKENS // TOK_GRP)
    routes_turns = jax.random.permutation(jax.random.fold_in(keys[4], 3), STEPS * 2 * N_PIPE * TOKENS // TOK_GRP)
    routes = jax.vmap(lambda own, number: shared_out(jax.random.fold_in(keys[4], 2), own, number, TOK_GRP, GROUPS, TOPK, CAP, 2))(routes_keys, routes_turns).reshape((STEPS, 2, N_PIPE, TOKENS, TOPK))
    route_weight = jnp.clip(jnp.exp(math.log(1.0) - 2.3025851 * jax.random.uniform(keys[5], (STEPS, 2, N_PIPE, TOKENS, TOPK), jnp.float32) ** steps_of(keys[5], (STEPS, 2, N_PIPE, TOKENS, TOPK), ((2, 8),), -0.2, 0.2)), 0.1, 1.0)
    return {"state": state, "up_weight": up_weight, "down_weight": down_weight, "norm_gain": norm_gain, "routes": routes, "route_weight": route_weight}


def to_rows(blocks):
    grid = blocks.reshape(GROUPS, SLICES, TOK_GRP, DS)
    return grid.transpose(0, 2, 1, 3).reshape(TOKENS, D)

def to_blocks(rows):
    grid = rows.reshape(GROUPS, TOK_GRP, SLICES, DS)
    return grid.transpose(0, 2, 1, 3).reshape(N_EXPERT, TOK_GRP, DS)

def section_layer(blocks, gain, up_all, down_all, chosen, weights):
    xrows = to_rows(blocks)
    xf = xrows.astype(jnp.float32)
    meansq = lax.optimization_barrier(jnp.mean(xf * xf, axis=1, keepdims=True))
    normed = (xf * lax.rsqrt(meansq + 1e-06) * gain[None, :]).astype(jnp.bfloat16)
    expert_ids = jnp.arange(GROUPS, dtype=jnp.int32)
    hits = lax.optimization_barrier(jnp.sum((chosen[:, :, None] == expert_ids[None, None, :]).astype(jnp.int32), axis=1))
    hitg = hits.reshape(GROUPS, TOK_GRP, GROUPS)
    ranks = jnp.cumsum(hitg, axis=1) - hitg
    slot_ids = jnp.arange(CAP, dtype=jnp.int32)
    placed = jnp.where((hitg[..., None] == 1) & (ranks[..., None] == slot_ids), 1.0, 0.0).astype(jnp.float32)
    mixw = lax.optimization_barrier(jnp.sum(weights[:, :, None] * (chosen[:, :, None] == expert_ids[None, None, :]).astype(jnp.float32), axis=1))
    mixw = mixw.reshape(GROUPS, TOK_GRP, GROUPS)
    ups = up_all.reshape(GROUPS, D, FFW)
    downs = down_all.reshape(GROUPS, SLICES, FFW, DS).transpose(0, 2, 1, 3).reshape(GROUPS, FFW, D)
    normg = normed.reshape(GROUPS, TOK_GRP, D).astype(jnp.float32)

    def one_expert(index):
        sel = placed[:, :, index, :]
        picked = jnp.einsum('gtc,gtd->gcd', sel, normg).astype(jnp.bfloat16).reshape(GROUPS * CAP, D)
        upper = jnp.dot(picked, ups[index], preferred_element_type=jnp.float32)
        hidden = jax.nn.silu(upper).astype(jnp.bfloat16)
        return jnp.dot(hidden, downs[index], preferred_element_type=jnp.float32).astype(jnp.bfloat16).reshape(GROUPS, CAP, D)
    outputs = lax.map(one_expert, jnp.arange(GROUPS, dtype=jnp.int32))
    combine = placed * mixw[..., None]
    mixed = jnp.einsum('gtjc,jgcd->gtd', combine, outputs.astype(jnp.float32), precision=lax.Precision.HIGHEST)
    result = (xf + mixed.reshape(TOKENS, D)).astype(jnp.bfloat16)
    return to_blocks(result)

def reference(state, up_weight, down_weight, norm_gain, routes, route_weight):
    current = state
    for step in range(STEPS):

        def run_one(index):
            section = index // 2
            stream = index % 2
            return section_layer(current[section, stream], norm_gain[section], up_weight[section], down_weight[section], routes[step, stream, section], route_weight[step, stream, section])
        results = lax.map(run_one, jnp.arange(2 * N_PIPE, dtype=jnp.int32)).reshape(N_PIPE, 2, N_EXPERT, TOK_GRP, DS)
        forward = jnp.roll(results[:, 0], 1, axis=0)
        backward = jnp.roll(results[:, 1], -1, axis=0)
        current = jnp.stack([forward, backward], axis=1)
    return current
```

```python
import jax
import jax.numpy as jnp
from jax import lax
from jax.sharding import PartitionSpec as P

GROUPS = 8
SLICES = 8
CAP = 8


def over_groups(value):
    members = [[g * SLICES + s for g in range(GROUPS)] for s in range(SLICES)]
    return lax.all_to_all(value, "expert", 0, 0, axis_index_groups=members, tiled=True)


def over_slices(value):
    members = [[g * SLICES + s for s in range(SLICES)] for g in range(GROUPS)]
    return lax.all_to_all(value, "expert", 0, 0, axis_index_groups=members, tiled=True)


def shifted(value, steps):
    count = lax.axis_size("pipe")
    return lax.ppermute(value, "pipe", [(i, (i + steps) % count) for i in range(count)])


def slot_matrices(chosen, weights):
    streams, tokens, _ = chosen.shape
    expert_ids = jnp.arange(GROUPS, dtype=jnp.int32)
    matches = chosen[:, :, :, None] == expert_ids
    hits = jnp.sum(matches.astype(jnp.int32), axis=2)
    ranks = jnp.cumsum(hits, axis=1) - hits
    mixw = jnp.sum(jnp.where(matches, weights[..., None], 0.0), axis=2)
    slot_ids = jnp.arange(CAP, dtype=jnp.int32)
    placed = (hits[..., None] == 1) & (ranks[..., None] == slot_ids)
    same = jnp.eye(streams, dtype=jnp.bool_)
    full = placed[:, :, :, None, :] & same[:, None, None, :, None]
    full = full.reshape(streams * tokens, GROUPS * streams * CAP)
    mixed = jnp.broadcast_to(
        mixw[:, :, :, None, None], (streams, tokens, GROUPS, streams, CAP)
    ).reshape(full.shape)
    return full.astype(jnp.bfloat16), jnp.where(full, mixed, 0.0)


def shards(state, up_weight, down_weight, norm_gain, routes, route_weight):
    expert_index = lax.axis_index("expert")
    group_id = expert_index // SLICES
    slice_id = expert_index % SLICES
    streams, tokens, width = state.shape[1], state.shape[3], state.shape[4]
    features = width * SLICES
    up, down = up_weight[0, 0], down_weight[0, 0]
    hidden_width = up.shape[1]
    gain = lax.dynamic_slice_in_dim(norm_gain[0], slice_id * width, width, 0)
    lane = jnp.arange(128)
    current = state[0, :, 0].reshape(streams * tokens, width)
    slots = streams * CAP
    for step in range(routes.shape[0]):
        chosen = lax.dynamic_slice_in_dim(routes[step, :, 0], group_id * tokens, tokens, 1)
        weights = lax.dynamic_slice_in_dim(route_weight[step, :, 0], group_id * tokens, tokens, 1)
        placed, mix = slot_matrices(chosen, weights)
        outgoing = lax.dot_general(
            placed, current, (((0,), (0,)), ((), ())), preferred_element_type=jnp.float32
        ).astype(jnp.bfloat16)
        rows = over_groups(outgoing.reshape(GROUPS, slots, width)).reshape(GROUPS * slots, width)
        rows_f = rows.astype(jnp.float32)
        squares = jnp.sum(rows_f * rows_f, axis=1, keepdims=True)
        scaled = (rows_f * gain).astype(jnp.bfloat16)
        partial = jnp.dot(scaled, up, preferred_element_type=jnp.float32).astype(jnp.bfloat16)
        high = lax.reduce_precision(squares, 8, 7)
        tail = jnp.where(lane == 0, high, jnp.where(lane == 1, squares - high, 0.0))
        sent = jnp.concatenate([partial, tail.astype(jnp.bfloat16)], axis=1)
        parts = over_slices(sent.reshape(SLICES, slots, hidden_width + 128)).astype(jnp.float32)
        total = jnp.sum(parts, axis=0)
        summed = total[:, hidden_width : hidden_width + 1] + total[:, hidden_width + 1 : hidden_width + 2]
        value = total[:, :hidden_width] * lax.rsqrt(summed / features + 1e-06)
        active = jax.nn.silu(value).astype(jnp.bfloat16)
        hidden = over_slices(jnp.broadcast_to(active, (SLICES, slots, hidden_width)))
        produced = jnp.dot(
            hidden.reshape(GROUPS * slots, hidden_width), down, preferred_element_type=jnp.float32
        ).astype(jnp.bfloat16)
        returned = over_groups(produced.reshape(GROUPS, slots, width)).reshape(GROUPS * slots, width)
        added = jnp.dot(
            mix,
            returned.astype(jnp.float32),
            precision=lax.Precision.HIGHEST,
            preferred_element_type=jnp.float32,
        )
        result = (current.astype(jnp.float32) + added).astype(jnp.bfloat16)
        forward = shifted(result[:tokens], 1)
        backward = shifted(result[tokens:], -1)
        current = jnp.concatenate([forward, backward], axis=0)
    return current.reshape(1, streams, 1, tokens, width)


def solution(mesh):
    return jax.shard_map(
        shards,
        mesh=mesh,
        in_specs=(
            P("pipe", None, "expert", None, None),
            P("pipe", "expert", None, None),
            P("pipe", "expert", None, None),
            P("pipe", None),
            P(None, None, "pipe", None, None),
            P(None, None, "pipe", None, None),
        ),
        out_specs=P("pipe", None, "expert", None, None),
        check_vma=False,
    )
```

```python
import jax
import jax.numpy as jnp
from jax import lax
from jax.experimental import pallas as pl
from jax.experimental.pallas import tpu as pltpu
from jax.sharding import PartitionSpec as P

GROUPS = 8
SLICES = 8
CAP = 8
LANES = 128
VMEM = pl.BlockSpec(memory_space=pltpu.VMEM)
HBM = pl.BlockSpec(memory_space=pltpu.HBM)


def over_groups(value):
    members = [[g * SLICES + s for g in range(GROUPS)] for s in range(SLICES)]
    return lax.all_to_all(value, "expert", 0, 0, axis_index_groups=members, tiled=True)


def over_slices(value):
    members = [[g * SLICES + s for s in range(SLICES)] for g in range(GROUPS)]
    return lax.all_to_all(value, "expert", 0, 0, axis_index_groups=members, tiled=True)


def shifted(value, steps):
    count = lax.axis_size("pipe")
    return lax.ppermute(value, "pipe", [(i, (i + steps) % count) for i in range(count)])


def prepare(
    state_hbm, routes_hbm, weights_hbm, gain_hbm,
    rows_ref, place_ref, mix_ref, gain_ref,
    state_ref, routes_ref, weights_ref, arrived,
):
    expert_index = lax.axis_index("expert")
    group, part = expert_index // SLICES, expert_index % SLICES
    steps, streams, topk, every = routes_ref.shape
    tokens = every // GROUPS
    slots = GROUPS * streams * CAP
    width = state_ref.shape[1]
    own_gain = gain_hbm.at[:, pl.ds(pl.multiple_of(part * width, LANES), width)]
    copies = [
        pltpu.make_async_copy(source, target, arrived.at[i])
        for i, (source, target) in enumerate(
            [
                (routes_hbm, routes_ref),
                (weights_hbm, weights_ref),
                (state_hbm, state_ref),
                (own_gain, gain_ref),
            ]
        )
    ]
    for copy in copies:
        copy.start()

    def own(ref, step, choice):
        lane = lax.broadcasted_iota(jnp.int32, (1, every), 1)
        out = jnp.zeros((1, every), ref.dtype)
        for m in range(streams):
            line = ref[step, m, choice : choice + 1, :]
            line = pltpu.roll(line, (every - group * tokens + m * tokens) % every, 1)
            out = jnp.where(lane // tokens == m, line, out)
        return out

    row = lax.broadcasted_iota(jnp.int32, (slots, every), 0)
    lane = lax.broadcasted_iota(jnp.int32, (slots, every), 1)
    expert, stream, slot = row // (streams * CAP), row // CAP % streams, row % CAP
    mine = lane // tokens == stream
    earlier_row = lax.broadcasted_iota(jnp.int32, (every, every), 0)
    earlier_lane = lax.broadcasted_iota(jnp.int32, (every, every), 1)
    earlier = (earlier_row // tokens == earlier_lane // tokens) & (earlier_row < earlier_lane)
    earlier = jnp.where(earlier, 1.0, 0.0).astype(jnp.bfloat16)
    for copy in copies:
        copy.wait()
    for step in range(steps):
        named = [mine & (own(routes_ref, step, k) == expert) for k in range(topk)]
        hit = named[0]
        for k in range(1, topk):
            hit = hit | named[k]
        hit = jnp.where(hit, 1.0, 0.0)
        rank = jnp.dot(hit.astype(jnp.bfloat16), earlier, preferred_element_type=jnp.float32)
        placed = jnp.where(rank == slot.astype(jnp.float32), hit, 0.0)
        weight = jnp.zeros((slots, every), jnp.float32)
        for k in range(topk):
            weight = jnp.where(named[k], own(weights_ref, step, k), weight)
        mix = jnp.transpose(placed * weight)
        mix_ref[step] = mix[: streams * tokens]
        narrow = placed[:, : streams * tokens].astype(jnp.bfloat16)
        if step == 0:
            rows_ref[...] = jnp.dot(
                narrow, state_ref[...], preferred_element_type=jnp.float32
            ).astype(jnp.bfloat16)
        else:
            place_ref[step - 1] = narrow


def shards(state, up_weight, down_weight, norm_gain, routes, route_weight):
    streams, tokens, width = state.shape[1], state.shape[3], state.shape[4]
    steps = routes.shape[0]
    features = width * SLICES
    up, down = up_weight[0, 0], down_weight[0, 0]
    hidden_width = up.shape[1]
    slots = streams * CAP
    current = state[0, :, 0].reshape(streams * tokens, width)
    outgoing, place, mix, gain = pl.pallas_call(
        prepare,
        out_shape=(
            jax.ShapeDtypeStruct((GROUPS * slots, width), jnp.bfloat16),
            jax.ShapeDtypeStruct((steps - 1, GROUPS * slots, streams * tokens), jnp.bfloat16),
            jax.ShapeDtypeStruct((steps, streams * tokens, GROUPS * slots), jnp.float32),
            jax.ShapeDtypeStruct((1, width), jnp.float32),
        ),
        in_specs=[HBM, HBM, HBM, HBM],
        out_specs=(VMEM, VMEM, VMEM, VMEM),
        scratch_shapes=[
            pltpu.VMEM(current.shape, current.dtype),
            pltpu.VMEM((steps, streams, routes.shape[4], routes.shape[3]), routes.dtype),
            pltpu.VMEM((steps, streams, routes.shape[4], routes.shape[3]), route_weight.dtype),
            pltpu.SemaphoreType.DMA((4,)),
        ],
        name="prepare",
    )(
        current,
        jnp.swapaxes(routes[:, :, 0], 2, 3),
        jnp.swapaxes(route_weight[:, :, 0], 2, 3),
        norm_gain,
    )
    lane = jnp.arange(LANES)
    for step in range(steps):
        if step > 0:
            outgoing = jnp.dot(
                place[step - 1], current, preferred_element_type=jnp.float32
            ).astype(jnp.bfloat16)
        rows = over_groups(outgoing.reshape(GROUPS, slots, width)).reshape(GROUPS * slots, width)
        rows_f = rows.astype(jnp.float32)
        squares = jnp.sum(rows_f * rows_f, axis=1, keepdims=True)
        scaled = (rows_f * gain).astype(jnp.bfloat16)
        partial = jnp.dot(scaled, up, preferred_element_type=jnp.float32).astype(jnp.bfloat16)
        high = lax.reduce_precision(squares, 8, 7)
        tail = jnp.where(lane == 0, high, jnp.where(lane == 1, squares - high, 0.0))
        sent = jnp.concatenate([partial, tail.astype(jnp.bfloat16)], axis=1)
        parts = over_slices(sent.reshape(SLICES, slots, hidden_width + LANES)).astype(jnp.float32)
        total = jnp.sum(parts, axis=0)
        summed = total[:, hidden_width : hidden_width + 1] + total[:, hidden_width + 1 : hidden_width + 2]
        value = total[:, :hidden_width] * lax.rsqrt(summed / features + 1e-06)
        active = jax.nn.silu(value).astype(jnp.bfloat16)
        hidden = over_slices(jnp.broadcast_to(active, (SLICES, slots, hidden_width)))
        produced = jnp.dot(
            hidden.reshape(GROUPS * slots, hidden_width), down, preferred_element_type=jnp.float32
        ).astype(jnp.bfloat16)
        returned = over_groups(produced.reshape(GROUPS, slots, width)).reshape(GROUPS * slots, width)
        added = jnp.dot(
            mix[step],
            returned.astype(jnp.float32),
            precision=lax.Precision.HIGHEST,
            preferred_element_type=jnp.float32,
        )
        result = (current.astype(jnp.float32) + added).astype(jnp.bfloat16)
        forward = shifted(result[:tokens], 1)
        backward = shifted(result[tokens:], -1)
        current = jnp.concatenate([forward, backward], axis=0)
    return current.reshape(1, streams, 1, tokens, width)


def solution(mesh):
    return jax.shard_map(
        shards,
        mesh=mesh,
        in_specs=(
            P("pipe", None, "expert", None, None),
            P("pipe", "expert", None, None),
            P("pipe", "expert", None, None),
            P("pipe", None),
            P(None, None, "pipe", None, None),
            P(None, None, "pipe", None, None),
        ),
        out_specs=P("pipe", None, "expert", None, None),
        check_vma=False,
    )
```

```python
import jax
import jax.numpy as jnp
from jax import lax
from jax.experimental import pallas as pl
from jax.experimental.pallas import tpu as pltpu
from jax.sharding import PartitionSpec as P

GROUPS = 8
SLICES = 8
CAP = 8
LANES = 128
VMEM = pl.BlockSpec(memory_space=pltpu.VMEM)
HBM = pl.BlockSpec(memory_space=pltpu.HBM)


def over_groups(value):
    members = [[g * SLICES + s for g in range(GROUPS)] for s in range(SLICES)]
    return lax.all_to_all(value, "expert", 0, 0, axis_index_groups=members, tiled=True)


def over_slices(value):
    members = [[g * SLICES + s for s in range(SLICES)] for g in range(GROUPS)]
    return lax.all_to_all(value, "expert", 0, 0, axis_index_groups=members, tiled=True)


def swapped(value, off_chip):
    count = lax.axis_size("pipe")
    pairs = [(i, i ^ 1) for i in range(count)]
    if off_chip:
        pairs = [(i, (i + 1 if i % 2 else i - 1) % count) for i in range(count)]
    return lax.ppermute(value, "pipe", pairs)


def prepare(
    state_hbm, routes_hbm, weights_hbm, gain_hbm,
    rows_ref, state_ref, place_ref, mix_ref, gain_ref,
    routes_ref, weights_ref, gain_line, arrived,
):
    expert_index = lax.axis_index("expert")
    odd = lax.axis_index("pipe") % 2
    group, part = expert_index // SLICES, expert_index % SLICES
    steps, streams, topk, every = routes_ref.shape
    tokens = every // GROUPS
    slots = GROUPS * streams * CAP
    width = state_ref.shape[1]
    stream_at = [odd, 1 - odd]
    own_gain = gain_hbm.at[:, pl.ds(pl.multiple_of(part * width, LANES), width)]
    moves = [(routes_hbm, routes_ref), (weights_hbm, weights_ref), (own_gain, gain_line)]
    for q in range(streams):
        moves.append((state_hbm.at[stream_at[q]], state_ref.at[pl.ds(q * tokens, tokens)]))
    copies = [
        pltpu.make_async_copy(source, target, arrived.at[i])
        for i, (source, target) in enumerate(moves)
    ]
    for copy in copies:
        copy.start()

    def own(ref, step, choice):
        lane = lax.broadcasted_iota(jnp.int32, (1, every), 1)
        out = jnp.zeros((1, every), ref.dtype)
        for q in range(streams):
            line = ref[step, stream_at[q], choice : choice + 1, :]
            line = pltpu.roll(line, (every - group * tokens + q * tokens) % every, 1)
            out = jnp.where(lane // tokens == q, line, out)
        return out

    row = lax.broadcasted_iota(jnp.int32, (slots, every), 0)
    lane = lax.broadcasted_iota(jnp.int32, (slots, every), 1)
    expert, position, slot = row // (streams * CAP), row // CAP % streams, row % CAP
    mine = lane // tokens == position
    earlier_row = lax.broadcasted_iota(jnp.int32, (every, every), 0)
    earlier_lane = lax.broadcasted_iota(jnp.int32, (every, every), 1)
    earlier = (earlier_row // tokens == earlier_lane // tokens) & (earlier_row < earlier_lane)
    earlier = jnp.where(earlier, 1.0, 0.0).astype(jnp.bfloat16)
    for copy in copies:
        copy.wait()
    gain_ref[...] = jnp.broadcast_to(gain_line[...], gain_ref.shape)
    for step in range(steps):
        named = [mine & (own(routes_ref, step, k) == expert) for k in range(topk)]
        hit = named[0]
        for k in range(1, topk):
            hit = hit | named[k]
        hit = jnp.where(hit, 1.0, 0.0)
        rank = jnp.dot(hit.astype(jnp.bfloat16), earlier, preferred_element_type=jnp.float32)
        placed = jnp.where(rank == slot.astype(jnp.float32), hit, 0.0)
        weight = jnp.zeros((slots, every), jnp.float32)
        for k in range(topk):
            weight = jnp.where(named[k], own(weights_ref, step, k), weight)
        mix = jnp.transpose(placed * weight)
        mix_ref[step] = mix[: streams * tokens]
        narrow = placed[:, : streams * tokens].astype(jnp.bfloat16)
        if step == 0:
            rows_ref[...] = jnp.dot(
                narrow, state_ref[...], preferred_element_type=jnp.float32
            ).astype(jnp.bfloat16)
        else:
            place_ref[step - 1] = narrow


def shards(state, up_weight, down_weight, norm_gain, routes, route_weight):
    streams, tokens, width = state.shape[1], state.shape[3], state.shape[4]
    steps = routes.shape[0]
    features = width * SLICES
    up, down = up_weight[0, 0], down_weight[0, 0]
    hidden_width = up.shape[1]
    slots = streams * CAP
    outgoing, current, place, mix, gain = pl.pallas_call(
        prepare,
        out_shape=(
            jax.ShapeDtypeStruct((GROUPS * slots, width), jnp.bfloat16),
            jax.ShapeDtypeStruct((streams * tokens, width), state.dtype),
            jax.ShapeDtypeStruct((steps - 1, GROUPS * slots, streams * tokens), jnp.bfloat16),
            jax.ShapeDtypeStruct((steps, streams * tokens, GROUPS * slots), jnp.float32),
            jax.ShapeDtypeStruct((slots, width), jnp.float32),
        ),
        in_specs=[HBM, HBM, HBM, HBM],
        out_specs=(VMEM, VMEM, VMEM, VMEM, VMEM),
        scratch_shapes=[
            pltpu.VMEM((steps, streams, routes.shape[4], routes.shape[3]), routes.dtype),
            pltpu.VMEM((steps, streams, routes.shape[4], routes.shape[3]), route_weight.dtype),
            pltpu.VMEM((1, width), jnp.float32),
            pltpu.SemaphoreType.DMA((5,)),
        ],
        name="prepare",
    )(
        state[0, :, 0],
        jnp.swapaxes(routes[:, :, 0], 2, 3),
        jnp.swapaxes(route_weight[:, :, 0], 2, 3),
        norm_gain,
    )
    lane = jnp.arange(LANES)
    for step in range(steps):
        if step > 0:
            outgoing = jnp.dot(
                place[step - 1], current, preferred_element_type=jnp.float32
            ).astype(jnp.bfloat16)
        rows_f = over_groups(outgoing.reshape(GROUPS, slots, width)).astype(jnp.float32)
        squares = jnp.sum(rows_f * rows_f, axis=2).reshape(GROUPS * slots, 1)
        scaled = (rows_f * gain).astype(jnp.bfloat16).reshape(GROUPS * slots, width)
        partial = jnp.dot(scaled, up, preferred_element_type=jnp.float32).astype(jnp.bfloat16)
        high = lax.reduce_precision(squares, 8, 7)
        tail = jnp.where(lane == 0, high, jnp.where(lane == 1, squares - high, 0.0))
        sent = jnp.concatenate([partial, tail.astype(jnp.bfloat16)], axis=1)
        parts = over_slices(sent.reshape(SLICES, slots, hidden_width + LANES)).astype(jnp.float32)
        total = jnp.sum(parts, axis=0)
        summed = total[:, hidden_width : hidden_width + 1] + total[:, hidden_width + 1 : hidden_width + 2]
        value = total[:, :hidden_width] * lax.rsqrt(summed / features + 1e-06)
        active = jax.nn.silu(value).astype(jnp.bfloat16)
        hidden = over_slices(jnp.broadcast_to(active, (SLICES, slots, hidden_width)))
        produced = jnp.dot(
            hidden.reshape(GROUPS * slots, hidden_width), down, preferred_element_type=jnp.float32
        ).astype(jnp.bfloat16)
        returned = over_groups(produced.reshape(GROUPS, slots, width)).reshape(GROUPS * slots, width)
        added = jnp.dot(
            mix[step],
            returned.astype(jnp.float32),
            precision=lax.Precision.HIGHEST,
            preferred_element_type=jnp.float32,
        )
        result = (current.astype(jnp.float32) + added).astype(jnp.bfloat16)
        far = swapped(result[tokens:], True)
        near = swapped(result[:tokens], False)
        current = jnp.concatenate([far, near], axis=0)
    odd = lax.axis_index("pipe") % 2 == 1
    ordered = jnp.stack([jnp.where(odd, near, far), jnp.where(odd, far, near)])
    return ordered[None, :, None]


def solution(mesh):
    return jax.shard_map(
        shards,
        mesh=mesh,
        in_specs=(
            P("pipe", None, "expert", None, None),
            P("pipe", "expert", None, None),
            P("pipe", "expert", None, None),
            P("pipe", None),
            P(None, None, "pipe", None, None),
            P(None, None, "pipe", None, None),
        ),
        out_specs=P("pipe", None, "expert", None, None),
        check_vma=False,
    )
```

```python
import jax
import jax.numpy as jnp
from jax import lax
from jax.experimental import pallas as pl
from jax.experimental.pallas import tpu as pltpu
from jax.sharding import PartitionSpec as P

GROUPS = 8
SLICES = 8
CAP = 8
LANES = 128
FIRST = 5
VMEM = pl.BlockSpec(memory_space=pltpu.VMEM)
HBM = pl.BlockSpec(memory_space=pltpu.HBM)


def over_groups(value):
    order = [(i + FIRST) % GROUPS for i in range(GROUPS)]
    members = [[g * SLICES + s for g in order] for s in range(SLICES)]
    return lax.all_to_all(value, "expert", 0, 0, axis_index_groups=members, tiled=True)


def over_slices(value):
    members = [[g * SLICES + s for s in range(SLICES)] for g in range(GROUPS)]
    return lax.all_to_all(value, "expert", 0, 0, axis_index_groups=members, tiled=True)


def shifted(value, steps):
    count = lax.axis_size("pipe")
    return lax.ppermute(value, "pipe", [(i, (i + steps) % count) for i in range(count)])


def prepare(
    state_hbm, routes_hbm, weights_hbm, gain_hbm,
    rows_ref, place_ref, mix_ref, gain_ref,
    state_ref, routes_ref, weights_ref, arrived,
):
    expert_index = lax.axis_index("expert")
    group, part = expert_index // SLICES, expert_index % SLICES
    steps, streams, topk, every = routes_ref.shape
    tokens = every // GROUPS
    slots = GROUPS * streams * CAP
    width = state_ref.shape[1]
    own_gain = gain_hbm.at[:, pl.ds(pl.multiple_of(part * width, LANES), width)]
    copies = [
        pltpu.make_async_copy(source, target, arrived.at[i])
        for i, (source, target) in enumerate(
            [
                (routes_hbm, routes_ref),
                (weights_hbm, weights_ref),
                (state_hbm, state_ref),
                (own_gain, gain_ref),
            ]
        )
    ]
    for copy in copies:
        copy.start()

    def own(ref, step, choice):
        lane = lax.broadcasted_iota(jnp.int32, (1, every), 1)
        out = jnp.zeros((1, every), ref.dtype)
        for m in range(streams):
            line = ref[step, m, choice : choice + 1, :]
            line = pltpu.roll(line, (every - group * tokens + m * tokens) % every, 1)
            out = jnp.where(lane // tokens == m, line, out)
        return out

    row = lax.broadcasted_iota(jnp.int32, (slots, every), 0)
    lane = lax.broadcasted_iota(jnp.int32, (slots, every), 1)
    expert = (row // (streams * CAP) + FIRST) % GROUPS
    stream, slot = row // CAP % streams, row % CAP
    mine = lane // tokens == stream
    earlier_row = lax.broadcasted_iota(jnp.int32, (every, every), 0)
    earlier_lane = lax.broadcasted_iota(jnp.int32, (every, every), 1)
    earlier = (earlier_row // tokens == earlier_lane // tokens) & (earlier_row < earlier_lane)
    earlier = jnp.where(earlier, 1.0, 0.0).astype(jnp.bfloat16)
    for copy in copies:
        copy.wait()
    for step in range(steps):
        named = [mine & (own(routes_ref, step, k) == expert) for k in range(topk)]
        hit = named[0]
        for k in range(1, topk):
            hit = hit | named[k]
        hit = jnp.where(hit, 1.0, 0.0)
        rank = jnp.dot(hit.astype(jnp.bfloat16), earlier, preferred_element_type=jnp.float32)
        placed = jnp.where(rank == slot.astype(jnp.float32), hit, 0.0)
        weight = jnp.zeros((slots, every), jnp.float32)
        for k in range(topk):
            weight = jnp.where(named[k], own(weights_ref, step, k), weight)
        mix = jnp.transpose(placed * weight)
        mix_ref[step] = mix[: streams * tokens]
        narrow = placed[:, : streams * tokens].astype(jnp.bfloat16)
        if step == 0:
            rows_ref[...] = jnp.dot(
                narrow, state_ref[...], preferred_element_type=jnp.float32
            ).astype(jnp.bfloat16)
        else:
            place_ref[step - 1] = narrow


def shards(state, up_weight, down_weight, norm_gain, routes, route_weight):
    streams, tokens, width = state.shape[1], state.shape[3], state.shape[4]
    steps = routes.shape[0]
    features = width * SLICES
    up, down = up_weight[0, 0], down_weight[0, 0]
    hidden_width = up.shape[1]
    slots = streams * CAP
    current = state[0, :, 0].reshape(streams * tokens, width)
    outgoing, place, mix, gain = pl.pallas_call(
        prepare,
        out_shape=(
            jax.ShapeDtypeStruct((GROUPS * slots, width), jnp.bfloat16),
            jax.ShapeDtypeStruct((steps - 1, GROUPS * slots, streams * tokens), jnp.bfloat16),
            jax.ShapeDtypeStruct((steps, streams * tokens, GROUPS * slots), jnp.float32),
            jax.ShapeDtypeStruct((1, width), jnp.float32),
        ),
        in_specs=[HBM, HBM, HBM, HBM],
        out_specs=(VMEM, VMEM, VMEM, VMEM),
        scratch_shapes=[
            pltpu.VMEM(current.shape, current.dtype),
            pltpu.VMEM((steps, streams, routes.shape[4], routes.shape[3]), routes.dtype),
            pltpu.VMEM((steps, streams, routes.shape[4], routes.shape[3]), route_weight.dtype),
            pltpu.SemaphoreType.DMA((4,)),
        ],
        name="prepare",
    )(
        current,
        jnp.swapaxes(routes[:, :, 0], 2, 3),
        jnp.swapaxes(route_weight[:, :, 0], 2, 3),
        norm_gain,
    )
    lane = jnp.arange(LANES)
    for step in range(steps):
        if step > 0:
            outgoing = jnp.dot(
                place[step - 1], current, preferred_element_type=jnp.float32
            ).astype(jnp.bfloat16)
        rows = over_groups(outgoing.reshape(GROUPS, slots, width)).reshape(GROUPS * slots, width)
        rows_f = rows.astype(jnp.float32)
        squares = jnp.sum(rows_f * rows_f, axis=1, keepdims=True)
        scaled = (rows_f * gain).astype(jnp.bfloat16)
        partial = jnp.dot(scaled, up, preferred_element_type=jnp.float32).astype(jnp.bfloat16)
        high = lax.reduce_precision(squares, 8, 7)
        tail = jnp.where(lane == 0, high, jnp.where(lane == 1, squares - high, 0.0))
        sent = jnp.concatenate([partial, tail.astype(jnp.bfloat16)], axis=1)
        parts = over_slices(sent.reshape(SLICES, slots, hidden_width + LANES)).astype(jnp.float32)
        total = jnp.sum(parts, axis=0)
        summed = total[:, hidden_width : hidden_width + 1] + total[:, hidden_width + 1 : hidden_width + 2]
        value = total[:, :hidden_width] * lax.rsqrt(summed / features + 1e-06)
        active = jax.nn.silu(value).astype(jnp.bfloat16)
        hidden = over_slices(jnp.broadcast_to(active, (SLICES, slots, hidden_width)))
        produced = jnp.dot(
            hidden.reshape(GROUPS * slots, hidden_width), down, preferred_element_type=jnp.float32
        ).astype(jnp.bfloat16)
        returned = over_groups(produced.reshape(GROUPS, slots, width)).reshape(GROUPS * slots, width)
        added = jnp.dot(
            mix[step],
            returned.astype(jnp.float32),
            precision=lax.Precision.HIGHEST,
            preferred_element_type=jnp.float32,
        )
        result = (current.astype(jnp.float32) + added).astype(jnp.bfloat16)
        forward = shifted(result[:tokens], 1)
        backward = shifted(result[tokens:], -1)
        current = jnp.concatenate([forward, backward], axis=0)
    return current.reshape(1, streams, 1, tokens, width)


def solution(mesh):
    return jax.shard_map(
        shards,
        mesh=mesh,
        in_specs=(
            P("pipe", None, "expert", None, None),
            P("pipe", "expert", None, None),
            P("pipe", "expert", None, None),
            P("pipe", None),
            P(None, None, "pipe", None, None),
            P(None, None, "pipe", None, None),
        ),
        out_specs=P("pipe", None, "expert", None, None),
        check_vma=False,
    )
```

```python
import jax
import jax.numpy as jnp
from jax import lax
from jax.experimental import pallas as pl
from jax.experimental.pallas import tpu as pltpu
from jax.sharding import PartitionSpec as P

GROUPS = 8
SLICES = 8
CAP = 8
LANES = 128
FIRST = 4
FIRST_SLICE = 3
VMEM = pl.BlockSpec(memory_space=pltpu.VMEM)
HBM = pl.BlockSpec(memory_space=pltpu.HBM)


def over_groups(value):
    order = [(i + FIRST) % GROUPS for i in range(GROUPS)]
    members = [[g * SLICES + s for g in order] for s in range(SLICES)]
    return lax.all_to_all(value, "expert", 0, 0, axis_index_groups=members, tiled=True)


def over_slices(value):
    order = [(i + FIRST_SLICE) % SLICES for i in range(SLICES)]
    members = [[g * SLICES + s for s in order] for g in range(GROUPS)]
    return lax.all_to_all(value, "expert", 0, 0, axis_index_groups=members, tiled=True)


def shifted(value, steps):
    count = lax.axis_size("pipe")
    return lax.ppermute(value, "pipe", [(i, (i + steps) % count) for i in range(count)])


def prepare(
    state_hbm, routes_hbm, weights_hbm, gain_hbm,
    rows_ref, place_ref, mix_ref, gain_ref,
    state_ref, routes_ref, weights_ref, arrived,
):
    expert_index = lax.axis_index("expert")
    group, part = expert_index // SLICES, expert_index % SLICES
    steps, streams, topk, every = routes_ref.shape
    tokens = every // GROUPS
    slots = GROUPS * streams * CAP
    width = state_ref.shape[1]
    own_gain = gain_hbm.at[:, pl.ds(pl.multiple_of(part * width, LANES), width)]
    copies = [
        pltpu.make_async_copy(source, target, arrived.at[i])
        for i, (source, target) in enumerate(
            [
                (routes_hbm, routes_ref),
                (weights_hbm, weights_ref),
                (state_hbm, state_ref),
                (own_gain, gain_ref),
            ]
        )
    ]
    for copy in copies:
        copy.start()

    def own(ref, step, choice):
        lane = lax.broadcasted_iota(jnp.int32, (1, every), 1)
        out = jnp.zeros((1, every), ref.dtype)
        for m in range(streams):
            line = ref[step, m, choice : choice + 1, :]
            line = pltpu.roll(line, (every - group * tokens + m * tokens) % every, 1)
            out = jnp.where(lane // tokens == m, line, out)
        return out

    row = lax.broadcasted_iota(jnp.int32, (slots, every), 0)
    lane = lax.broadcasted_iota(jnp.int32, (slots, every), 1)
    expert = (row // (streams * CAP) + FIRST) % GROUPS
    stream, slot = row // CAP % streams, row % CAP
    mine = lane // tokens == stream
    earlier_row = lax.broadcasted_iota(jnp.int32, (every, every), 0)
    earlier_lane = lax.broadcasted_iota(jnp.int32, (every, every), 1)
    earlier = (earlier_row // tokens == earlier_lane // tokens) & (earlier_row < earlier_lane)
    earlier = jnp.where(earlier, 1.0, 0.0).astype(jnp.bfloat16)
    for copy in copies:
        copy.wait()
    for step in range(steps):
        named = [mine & (own(routes_ref, step, k) == expert) for k in range(topk)]
        hit = named[0]
        for k in range(1, topk):
            hit = hit | named[k]
        hit = jnp.where(hit, 1.0, 0.0)
        rank = jnp.dot(hit.astype(jnp.bfloat16), earlier, preferred_element_type=jnp.float32)
        placed = jnp.where(rank == slot.astype(jnp.float32), hit, 0.0)
        weight = jnp.zeros((slots, every), jnp.float32)
        for k in range(topk):
            weight = jnp.where(named[k], own(weights_ref, step, k), weight)
        mix = jnp.transpose(placed * weight)
        mix_ref[step] = mix[: streams * tokens]
        narrow = placed[:, : streams * tokens].astype(jnp.bfloat16)
        if step == 0:
            rows_ref[...] = jnp.dot(
                narrow, state_ref[...], preferred_element_type=jnp.float32
            ).astype(jnp.bfloat16)
        else:
            place_ref[step - 1] = narrow


def shards(state, up_weight, down_weight, norm_gain, routes, route_weight):
    streams, tokens, width = state.shape[1], state.shape[3], state.shape[4]
    steps = routes.shape[0]
    features = width * SLICES
    up, down = up_weight[0, 0], down_weight[0, 0]
    hidden_width = up.shape[1]
    slots = streams * CAP
    current = state[0, :, 0].reshape(streams * tokens, width)
    outgoing, place, mix, gain = pl.pallas_call(
        prepare,
        out_shape=(
            jax.ShapeDtypeStruct((GROUPS * slots, width), jnp.bfloat16),
            jax.ShapeDtypeStruct((steps - 1, GROUPS * slots, streams * tokens), jnp.bfloat16),
            jax.ShapeDtypeStruct((steps, streams * tokens, GROUPS * slots), jnp.float32),
            jax.ShapeDtypeStruct((1, width), jnp.float32),
        ),
        in_specs=[HBM, HBM, HBM, HBM],
        out_specs=(VMEM, VMEM, VMEM, VMEM),
        scratch_shapes=[
            pltpu.VMEM(current.shape, current.dtype),
            pltpu.VMEM((steps, streams, routes.shape[4], routes.shape[3]), routes.dtype),
            pltpu.VMEM((steps, streams, routes.shape[4], routes.shape[3]), route_weight.dtype),
            pltpu.SemaphoreType.DMA((4,)),
        ],
        name="prepare",
    )(
        current,
        jnp.swapaxes(routes[:, :, 0], 2, 3),
        jnp.swapaxes(route_weight[:, :, 0], 2, 3),
        norm_gain,
    )
    lane = jnp.arange(LANES)
    for step in range(steps):
        if step > 0:
            outgoing = jnp.dot(
                place[step - 1], current, preferred_element_type=jnp.float32
            ).astype(jnp.bfloat16)
        rows = over_groups(outgoing.reshape(GROUPS, slots, width)).reshape(GROUPS * slots, width)
        rows_f = rows.astype(jnp.float32)
        squares = jnp.sum(rows_f * rows_f, axis=1, keepdims=True)
        scaled = (rows_f * gain).astype(jnp.bfloat16)
        partial = jnp.dot(scaled, up, preferred_element_type=jnp.float32).astype(jnp.bfloat16)
        high = lax.reduce_precision(squares, 8, 7)
        tail = jnp.where(lane == 0, high, jnp.where(lane == 1, squares - high, 0.0))
        sent = jnp.concatenate([partial, tail.astype(jnp.bfloat16)], axis=1)
        parts = over_slices(sent.reshape(SLICES, slots, hidden_width + LANES)).astype(jnp.float32)
        total = jnp.sum(parts, axis=0)
        summed = total[:, hidden_width : hidden_width + 1] + total[:, hidden_width + 1 : hidden_width + 2]
        value = total[:, :hidden_width] * lax.rsqrt(summed / features + 1e-06)
        active = jax.nn.silu(value).astype(jnp.bfloat16)
        hidden = over_slices(jnp.broadcast_to(active, (SLICES, slots, hidden_width)))
        produced = jnp.dot(
            hidden.reshape(GROUPS * slots, hidden_width), down, preferred_element_type=jnp.float32
        ).astype(jnp.bfloat16)
        returned = over_groups(produced.reshape(GROUPS, slots, width)).reshape(GROUPS * slots, width)
        added = jnp.dot(
            mix[step],
            returned.astype(jnp.float32),
            precision=lax.Precision.HIGHEST,
            preferred_element_type=jnp.float32,
        )
        result = (current.astype(jnp.float32) + added).astype(jnp.bfloat16)
        forward = shifted(result[:tokens], 1)
        backward = shifted(result[tokens:], -1)
        current = jnp.concatenate([forward, backward], axis=0)
    return current.reshape(1, streams, 1, tokens, width)


def solution(mesh):
    return jax.shard_map(
        shards,
        mesh=mesh,
        in_specs=(
            P("pipe", None, "expert", None, None),
            P("pipe", "expert", None, None),
            P("pipe", "expert", None, None),
            P("pipe", None),
            P(None, None, "pipe", None, None),
            P(None, None, "pipe", None, None),
        ),
        out_specs=P("pipe", None, "expert", None, None),
        check_vma=False,
    )
```

```python
import jax
import jax.numpy as jnp
from jax import lax
from jax.experimental import pallas as pl
from jax.experimental.pallas import tpu as pltpu
from jax.sharding import PartitionSpec as P

GROUPS = 8
SLICES = 8
CAP = 8
LANES = 128
FIRST = 4
FIRST_SLICE = 3
VMEM = pl.BlockSpec(memory_space=pltpu.VMEM)
HBM = pl.BlockSpec(memory_space=pltpu.HBM)


def over_groups(value):
    order = [(i + FIRST) % GROUPS for i in range(GROUPS)]
    members = [[g * SLICES + s for g in order] for s in range(SLICES)]
    return lax.all_to_all(value, "expert", 0, 0, axis_index_groups=members, tiled=True)


def over_slices(value):
    order = [(i + FIRST_SLICE) % SLICES for i in range(SLICES)]
    members = [[g * SLICES + s for s in order] for g in range(GROUPS)]
    return lax.all_to_all(value, "expert", 0, 0, axis_index_groups=members, tiled=True)


def shifted(value, steps):
    count = lax.axis_size("pipe")
    return lax.ppermute(value, "pipe", [(i, (i + steps) % count) for i in range(count)])


def prepare(
    state_hbm, routes_hbm, weights_hbm, gain_hbm,
    rows_ref, place_ref, mix_ref, gain_ref,
    state_ref, routes_ref, weights_ref, arrived,
):
    expert_index = lax.axis_index("expert")
    group, part = expert_index // SLICES, expert_index % SLICES
    steps, streams, topk, every = routes_ref.shape
    tokens = every // GROUPS
    slots = GROUPS * streams * CAP
    width = state_ref.shape[1]
    own_gain = gain_hbm.at[:, pl.ds(pl.multiple_of(part * width, LANES), width)]
    copies = [
        pltpu.make_async_copy(source, target, arrived.at[i])
        for i, (source, target) in enumerate(
            [
                (routes_hbm, routes_ref),
                (weights_hbm, weights_ref),
                (state_hbm, state_ref),
                (own_gain, gain_ref),
            ]
        )
    ]
    for copy in copies:
        copy.start()

    def own(ref, step, choice):
        lane = lax.broadcasted_iota(jnp.int32, (1, every), 1)
        out = jnp.zeros((1, every), ref.dtype)
        for m in range(streams):
            line = ref[step, m, choice : choice + 1, :]
            line = pltpu.roll(line, (every - group * tokens + m * tokens) % every, 1)
            out = jnp.where(lane // tokens == m, line, out)
        return out

    row = lax.broadcasted_iota(jnp.int32, (slots, every), 0)
    lane = lax.broadcasted_iota(jnp.int32, (slots, every), 1)
    expert = (row // (streams * CAP) + FIRST) % GROUPS
    stream, slot = row // CAP % streams, row % CAP
    mine = lane // tokens == stream
    earlier_row = lax.broadcasted_iota(jnp.int32, (every, every), 0)
    earlier_lane = lax.broadcasted_iota(jnp.int32, (every, every), 1)
    earlier = (earlier_row // tokens == earlier_lane // tokens) & (earlier_row < earlier_lane)
    earlier = jnp.where(earlier, 1.0, 0.0).astype(jnp.bfloat16)
    for copy in copies:
        copy.wait()
    for step in range(steps):
        named = [mine & (own(routes_ref, step, k) == expert) for k in range(topk)]
        hit = named[0]
        for k in range(1, topk):
            hit = hit | named[k]
        hit = jnp.where(hit, 1.0, 0.0)
        rank = jnp.dot(hit.astype(jnp.bfloat16), earlier, preferred_element_type=jnp.float32)
        placed = jnp.where(rank == slot.astype(jnp.float32), hit, 0.0)
        weight = jnp.zeros((slots, every), jnp.float32)
        for k in range(topk):
            weight = jnp.where(named[k], own(weights_ref, step, k), weight)
        mix = jnp.transpose(placed * weight)
        mix_ref[step] = mix[: streams * tokens]
        narrow = placed[:, : streams * tokens].astype(jnp.bfloat16)
        if step == 0:
            rows_ref[...] = jnp.dot(
                narrow, state_ref[...], preferred_element_type=jnp.float32
            ).astype(jnp.bfloat16)
        else:
            place_ref[step - 1] = narrow


def shards(state, up_weight, down_weight, norm_gain, routes, route_weight):
    streams, tokens, width = state.shape[1], state.shape[3], state.shape[4]
    steps = routes.shape[0]
    features = width * SLICES
    up, down = up_weight[0, 0], down_weight[0, 0]
    hidden_width = up.shape[1]
    slots = streams * CAP
    current = state[0, :, 0].reshape(streams * tokens, width)
    outgoing, place, mix, gain = pl.pallas_call(
        prepare,
        out_shape=(
            jax.ShapeDtypeStruct((GROUPS * slots, width), jnp.bfloat16),
            jax.ShapeDtypeStruct((steps - 1, GROUPS * slots, streams * tokens), jnp.bfloat16),
            jax.ShapeDtypeStruct((steps, streams * tokens, GROUPS * slots), jnp.float32),
            jax.ShapeDtypeStruct((1, width), jnp.float32),
        ),
        in_specs=[HBM, HBM, HBM, HBM],
        out_specs=(VMEM, VMEM, VMEM, VMEM),
        scratch_shapes=[
            pltpu.VMEM(current.shape, current.dtype),
            pltpu.VMEM((steps, streams, routes.shape[4], routes.shape[3]), routes.dtype),
            pltpu.VMEM((steps, streams, routes.shape[4], routes.shape[3]), route_weight.dtype),
            pltpu.SemaphoreType.DMA((4,)),
        ],
        name="prepare",
    )(
        current,
        jnp.swapaxes(routes[:, :, 0], 2, 3),
        jnp.swapaxes(route_weight[:, :, 0], 2, 3),
        norm_gain,
    )
    lane = jnp.arange(LANES)
    half = LANES // 2
    for step in range(steps):
        if step > 0:
            outgoing = jnp.dot(
                place[step - 1], current, preferred_element_type=jnp.float32
            ).astype(jnp.bfloat16)
        rows = over_groups(outgoing.reshape(GROUPS, slots, width)).reshape(GROUPS * slots, width)
        rows_f = rows.astype(jnp.float32)
        squares = jnp.sum(rows_f * rows_f, axis=1, keepdims=True)
        scaled = (rows_f * gain).astype(jnp.bfloat16)
        partial = jnp.dot(scaled, up, preferred_element_type=jnp.float32).astype(jnp.bfloat16)
        high = lax.reduce_precision(squares, 8, 7)
        tail = jnp.where(lane < half, high, squares - high)
        sent = jnp.concatenate([partial, tail.astype(jnp.bfloat16)], axis=1)
        parts = over_slices(sent.reshape(SLICES, slots, hidden_width + LANES)).astype(jnp.float32)
        total = jnp.sum(parts, axis=0)
        tails = total[:, hidden_width:]
        summed = tails + jnp.concatenate([tails[:, half:], tails[:, :half]], axis=1)
        scale = lax.rsqrt(summed / features + 1e-06)
        value = total[:, :hidden_width] * jnp.tile(scale, (1, hidden_width // LANES))
        active = jax.nn.silu(value).astype(jnp.bfloat16)
        hidden = over_slices(jnp.broadcast_to(active, (SLICES, slots, hidden_width)))
        produced = jnp.dot(
            hidden.reshape(GROUPS * slots, hidden_width), down, preferred_element_type=jnp.float32
        ).astype(jnp.bfloat16)
        returned = over_groups(produced.reshape(GROUPS, slots, width)).reshape(GROUPS * slots, width)
        added = jnp.dot(
            mix[step],
            returned.astype(jnp.float32),
            precision=lax.Precision.HIGHEST,
            preferred_element_type=jnp.float32,
        )
        result = (current.astype(jnp.float32) + added).astype(jnp.bfloat16)
        forward = shifted(result[:tokens], 1)
        backward = shifted(result[tokens:], -1)
        current = jnp.concatenate([forward, backward], axis=0)
    return current.reshape(1, streams, 1, tokens, width)


def solution(mesh):
    return jax.shard_map(
        shards,
        mesh=mesh,
        in_specs=(
            P("pipe", None, "expert", None, None),
            P("pipe", "expert", None, None),
            P("pipe", "expert", None, None),
            P("pipe", None),
            P(None, None, "pipe", None, None),
            P(None, None, "pipe", None, None),
        ),
        out_specs=P("pipe", None, "expert", None, None),
        check_vma=False,
    )
```

```python
import jax
import jax.numpy as jnp
from jax import lax
from jax.experimental import pallas as pl
from jax.experimental.pallas import tpu as pltpu
from jax.sharding import PartitionSpec as P

GROUPS = 8
SLICES = 8
CAP = 8
LANES = 128
FIRST = 6
FIRST_SLICE = 3
VMEM = pl.BlockSpec(memory_space=pltpu.VMEM)
HBM = pl.BlockSpec(memory_space=pltpu.HBM)


def over_groups(value, first):
    order = [(i + first) % GROUPS for i in range(GROUPS)]
    members = [[g * SLICES + s for g in order] for s in range(SLICES)]
    return lax.all_to_all(value, "expert", 0, 0, axis_index_groups=members, tiled=True)


def over_slices(value):
    order = [(i + FIRST_SLICE) % SLICES for i in range(SLICES)]
    members = [[g * SLICES + s for s in order] for g in range(GROUPS)]
    return lax.all_to_all(value, "expert", 0, 0, axis_index_groups=members, tiled=True)


def shifted(value, steps):
    count = lax.axis_size("pipe")
    return lax.ppermute(value, "pipe", [(i, (i + steps) % count) for i in range(count)])


def prepare(
    state_hbm, routes_hbm, weights_hbm, gain_hbm,
    rows_ref, place_ref, mix_ref, gain_ref,
    state_ref, routes_ref, weights_ref, arrived,
):
    expert_index = lax.axis_index("expert")
    group, part = expert_index // SLICES, expert_index % SLICES
    steps, streams, topk, every = routes_ref.shape
    tokens = every // GROUPS
    slots = GROUPS * streams * CAP
    width = state_ref.shape[1]
    own_gain = gain_hbm.at[:, pl.ds(pl.multiple_of(part * width, LANES), width)]
    copies = [
        pltpu.make_async_copy(source, target, arrived.at[i])
        for i, (source, target) in enumerate(
            [
                (routes_hbm, routes_ref),
                (weights_hbm, weights_ref),
                (state_hbm, state_ref),
                (own_gain, gain_ref),
            ]
        )
    ]
    for copy in copies:
        copy.start()

    def own(ref, step, choice):
        lane = lax.broadcasted_iota(jnp.int32, (1, every), 1)
        out = jnp.zeros((1, every), ref.dtype)
        for m in range(streams):
            line = ref[step, m, choice : choice + 1, :]
            line = pltpu.roll(line, (every - group * tokens + m * tokens) % every, 1)
            out = jnp.where(lane // tokens == m, line, out)
        return out

    row = lax.broadcasted_iota(jnp.int32, (slots, every), 0)
    lane = lax.broadcasted_iota(jnp.int32, (slots, every), 1)
    stream, slot = row // CAP % streams, row % CAP
    mine = lane // tokens == stream
    earlier_row = lax.broadcasted_iota(jnp.int32, (every, every), 0)
    earlier_lane = lax.broadcasted_iota(jnp.int32, (every, every), 1)
    earlier = (earlier_row // tokens == earlier_lane // tokens) & (earlier_row < earlier_lane)
    earlier = jnp.where(earlier, 1.0, 0.0).astype(jnp.bfloat16)
    for copy in copies:
        copy.wait()
    for step in range(steps):
        expert = (row // (streams * CAP) + (FIRST - step) % GROUPS) % GROUPS
        named = [mine & (own(routes_ref, step, k) == expert) for k in range(topk)]
        hit = named[0]
        for k in range(1, topk):
            hit = hit | named[k]
        hit = jnp.where(hit, 1.0, 0.0)
        rank = jnp.dot(hit.astype(jnp.bfloat16), earlier, preferred_element_type=jnp.float32)
        placed = jnp.where(rank == slot.astype(jnp.float32), hit, 0.0)
        weight = jnp.zeros((slots, every), jnp.float32)
        for k in range(topk):
            weight = jnp.where(named[k], own(weights_ref, step, k), weight)
        mix = jnp.transpose(pltpu.roll(placed * weight, streams * CAP, 0))
        mix_ref[step] = mix[: streams * tokens]
        narrow = placed[:, : streams * tokens].astype(jnp.bfloat16)
        if step == 0:
            rows_ref[...] = jnp.dot(
                narrow, state_ref[...], preferred_element_type=jnp.float32
            ).astype(jnp.bfloat16)
        else:
            place_ref[step - 1] = narrow


def shards(state, up_weight, down_weight, norm_gain, routes, route_weight):
    streams, tokens, width = state.shape[1], state.shape[3], state.shape[4]
    steps = routes.shape[0]
    features = width * SLICES
    up, down = up_weight[0, 0], down_weight[0, 0]
    hidden_width = up.shape[1]
    slots = streams * CAP
    current = state[0, :, 0].reshape(streams * tokens, width)
    outgoing, place, mix, gain = pl.pallas_call(
        prepare,
        out_shape=(
            jax.ShapeDtypeStruct((GROUPS * slots, width), jnp.bfloat16),
            jax.ShapeDtypeStruct((steps - 1, GROUPS * slots, streams * tokens), jnp.bfloat16),
            jax.ShapeDtypeStruct((steps, streams * tokens, GROUPS * slots), jnp.float32),
            jax.ShapeDtypeStruct((1, width), jnp.float32),
        ),
        in_specs=[HBM, HBM, HBM, HBM],
        out_specs=(VMEM, VMEM, VMEM, VMEM),
        scratch_shapes=[
            pltpu.VMEM(current.shape, current.dtype),
            pltpu.VMEM((steps, streams, routes.shape[4], routes.shape[3]), routes.dtype),
            pltpu.VMEM((steps, streams, routes.shape[4], routes.shape[3]), route_weight.dtype),
            pltpu.SemaphoreType.DMA((4,)),
        ],
        name="prepare",
    )(
        current,
        jnp.swapaxes(routes[:, :, 0], 2, 3),
        jnp.swapaxes(route_weight[:, :, 0], 2, 3),
        norm_gain,
    )
    lane = jnp.arange(LANES)
    half = LANES // 2
    for step in range(steps):
        first = (FIRST - step) % GROUPS
        if step > 0:
            outgoing = jnp.dot(
                place[step - 1], current, preferred_element_type=jnp.float32
            ).astype(jnp.bfloat16)
        rows = over_groups(outgoing.reshape(GROUPS, slots, width), first).reshape(GROUPS * slots, width)
        rows_f = rows.astype(jnp.float32)
        squares = jnp.sum(rows_f * rows_f, axis=1, keepdims=True)
        scaled = (rows_f * gain).astype(jnp.bfloat16)
        partial = jnp.dot(scaled, up, preferred_element_type=jnp.float32).astype(jnp.bfloat16)
        high = lax.reduce_precision(squares, 8, 7)
        tail = jnp.where(lane < half, high, squares - high)
        sent = jnp.concatenate([partial, tail.astype(jnp.bfloat16)], axis=1)
        sent = jnp.concatenate([sent[-slots:], sent[:-slots]], axis=0)
        parts = over_slices(sent.reshape(SLICES, slots, hidden_width + LANES)).astype(jnp.float32)
        total = jnp.sum(parts, axis=0)
        tails = total[:, hidden_width:]
        summed = tails + jnp.concatenate([tails[:, half:], tails[:, :half]], axis=1)
        scale = lax.rsqrt(summed / features + 1e-06)
        value = total[:, :hidden_width] * jnp.tile(scale, (1, hidden_width // LANES))
        active = jax.nn.silu(value).astype(jnp.bfloat16)
        hidden = over_slices(jnp.broadcast_to(active, (SLICES, slots, hidden_width)))
        produced = jnp.dot(
            hidden.reshape(GROUPS * slots, hidden_width), down, preferred_element_type=jnp.float32
        ).astype(jnp.bfloat16)
        returned = over_groups(produced.reshape(GROUPS, slots, width), first - 1).reshape(GROUPS * slots, width)
        added = jnp.dot(
            mix[step],
            returned.astype(jnp.float32),
            precision=lax.Precision.HIGHEST,
            preferred_element_type=jnp.float32,
        )
        result = (current.astype(jnp.float32) + added).astype(jnp.bfloat16)
        forward = shifted(result[:tokens], 1)
        backward = shifted(result[tokens:], -1)
        current = jnp.concatenate([forward, backward], axis=0)
    return current.reshape(1, streams, 1, tokens, width)


def solution(mesh):
    return jax.shard_map(
        shards,
        mesh=mesh,
        in_specs=(
            P("pipe", None, "expert", None, None),
            P("pipe", "expert", None, None),
            P("pipe", "expert", None, None),
            P("pipe", None),
            P(None, None, "pipe", None, None),
            P(None, None, "pipe", None, None),
        ),
        out_specs=P("pipe", None, "expert", None, None),
        check_vma=False,
    )
```

```python
import jax
import jax.numpy as jnp
from jax import lax
from jax.experimental import pallas as pl
from jax.experimental.pallas import tpu as pltpu
from jax.sharding import PartitionSpec as P

GROUPS = 8
SLICES = 8
CAP = 8
LANES = 128
FIRST = 5
FIRST_SLICE = 3
VMEM = pl.BlockSpec(memory_space=pltpu.VMEM)
HBM = pl.BlockSpec(memory_space=pltpu.HBM)


def over_groups(value, first):
    order = [(i + first) % GROUPS for i in range(GROUPS)]
    members = [[g * SLICES + s for g in order] for s in range(SLICES)]
    return lax.all_to_all(value, "expert", 0, 0, axis_index_groups=members, tiled=True)


def over_slices(value):
    order = [(i + FIRST_SLICE) % SLICES for i in range(SLICES)]
    members = [[g * SLICES + s for s in order] for g in range(GROUPS)]
    return lax.all_to_all(value, "expert", 0, 0, axis_index_groups=members, tiled=True)


def shifted(value, steps):
    count = lax.axis_size("pipe")
    return lax.ppermute(value, "pipe", [(i, (i + steps) % count) for i in range(count)])


def prepare(
    state_hbm, routes_hbm, weights_hbm, gain_hbm,
    rows_ref, place_ref, mix_ref, gain_ref,
    state_ref, routes_ref, weights_ref, arrived,
):
    expert_index = lax.axis_index("expert")
    group, part = expert_index // SLICES, expert_index % SLICES
    steps, streams, topk, every = routes_ref.shape
    tokens = every // GROUPS
    slots = GROUPS * streams * CAP
    width = state_ref.shape[1]
    own_gain = gain_hbm.at[:, pl.ds(pl.multiple_of(part * width, LANES), width)]
    copies = [
        pltpu.make_async_copy(source, target, arrived.at[i])
        for i, (source, target) in enumerate(
            [
                (routes_hbm, routes_ref),
                (weights_hbm, weights_ref),
                (state_hbm, state_ref),
                (own_gain, gain_ref),
            ]
        )
    ]
    for copy in copies:
        copy.start()

    def own(ref, step, choice):
        lane = lax.broadcasted_iota(jnp.int32, (1, every), 1)
        out = jnp.zeros((1, every), ref.dtype)
        for m in range(streams):
            line = ref[step, m, choice : choice + 1, :]
            line = pltpu.roll(line, (every - group * tokens + m * tokens) % every, 1)
            out = jnp.where(lane // tokens == m, line, out)
        return out

    row = lax.broadcasted_iota(jnp.int32, (slots, every), 0)
    lane = lax.broadcasted_iota(jnp.int32, (slots, every), 1)
    stream, slot = row // CAP % streams, row % CAP
    mine = lane // tokens == stream
    earlier_row = lax.broadcasted_iota(jnp.int32, (every, every), 0)
    earlier_lane = lax.broadcasted_iota(jnp.int32, (every, every), 1)
    earlier = (earlier_row // tokens == earlier_lane // tokens) & (earlier_row < earlier_lane)
    earlier = jnp.where(earlier, 1.0, 0.0).astype(jnp.bfloat16)
    for copy in copies:
        copy.wait()
    for step in range(steps):
        expert = (row // (streams * CAP) + FIRST) % GROUPS
        named = [mine & (own(routes_ref, step, k) == expert) for k in range(topk)]
        hit = named[0]
        for k in range(1, topk):
            hit = hit | named[k]
        hit = jnp.where(hit, 1.0, 0.0)
        rank = jnp.dot(hit.astype(jnp.bfloat16), earlier, preferred_element_type=jnp.float32)
        placed = jnp.where(rank == slot.astype(jnp.float32), hit, 0.0)
        weight = jnp.zeros((slots, every), jnp.float32)
        for k in range(topk):
            weight = jnp.where(named[k], own(weights_ref, step, k), weight)
        mix = jnp.transpose(pltpu.roll(placed * weight, streams * CAP, 0))
        mix_ref[step] = mix[: streams * tokens]
        narrow = placed[:, : streams * tokens].astype(jnp.bfloat16)
        if step == 0:
            rows_ref[...] = jnp.dot(
                narrow, state_ref[...], preferred_element_type=jnp.float32
            ).astype(jnp.bfloat16)
        else:
            place_ref[step - 1] = narrow


def shards(state, up_weight, down_weight, norm_gain, routes, route_weight):
    streams, tokens, width = state.shape[1], state.shape[3], state.shape[4]
    steps = routes.shape[0]
    features = width * SLICES
    up, down = up_weight[0, 0], down_weight[0, 0]
    hidden_width = up.shape[1]
    slots = streams * CAP
    current = state[0, :, 0].reshape(streams * tokens, width)
    outgoing, place, mix, gain = pl.pallas_call(
        prepare,
        out_shape=(
            jax.ShapeDtypeStruct((GROUPS * slots, width), jnp.bfloat16),
            jax.ShapeDtypeStruct((steps - 1, GROUPS * slots, streams * tokens), jnp.bfloat16),
            jax.ShapeDtypeStruct((steps, streams * tokens, GROUPS * slots), jnp.float32),
            jax.ShapeDtypeStruct((1, width), jnp.float32),
        ),
        in_specs=[HBM, HBM, HBM, HBM],
        out_specs=(VMEM, VMEM, VMEM, VMEM),
        scratch_shapes=[
            pltpu.VMEM(current.shape, current.dtype),
            pltpu.VMEM((steps, streams, routes.shape[4], routes.shape[3]), routes.dtype),
            pltpu.VMEM((steps, streams, routes.shape[4], routes.shape[3]), route_weight.dtype),
            pltpu.SemaphoreType.DMA((4,)),
        ],
        name="prepare",
    )(
        current,
        jnp.swapaxes(routes[:, :, 0], 2, 3),
        jnp.swapaxes(route_weight[:, :, 0], 2, 3),
        norm_gain,
    )
    lane = jnp.arange(LANES)
    half = LANES // 2
    for step in range(steps):
        first = FIRST
        if step > 0:
            outgoing = jnp.dot(
                place[step - 1], current, preferred_element_type=jnp.float32
            ).astype(jnp.bfloat16)
        rows = over_groups(outgoing.reshape(GROUPS, slots, width), first).reshape(GROUPS * slots, width)
        rows_f = rows.astype(jnp.float32)
        squares = jnp.sum(rows_f * rows_f, axis=1, keepdims=True)
        scaled = (rows_f * gain).astype(jnp.bfloat16)
        partial = jnp.dot(scaled, up, preferred_element_type=jnp.float32).astype(jnp.bfloat16)
        high = lax.reduce_precision(squares, 8, 7)
        tail = jnp.where(lane < half, high, squares - high)
        sent = jnp.concatenate([partial, tail.astype(jnp.bfloat16)], axis=1)
        sent = jnp.concatenate([sent[-slots:], sent[:-slots]], axis=0)
        parts = over_slices(sent.reshape(SLICES, slots, hidden_width + LANES)).astype(jnp.float32)
        total = jnp.sum(parts, axis=0)
        tails = total[:, hidden_width:]
        summed = tails + jnp.concatenate([tails[:, half:], tails[:, :half]], axis=1)
        scale = lax.rsqrt(summed / features + 1e-06)
        value = total[:, :hidden_width] * jnp.tile(scale, (1, hidden_width // LANES))
        active = jax.nn.silu(value).astype(jnp.bfloat16)
        hidden = over_slices(jnp.broadcast_to(active, (SLICES, slots, hidden_width)))
        produced = jnp.dot(
            hidden.reshape(GROUPS * slots, hidden_width), down, preferred_element_type=jnp.float32
        ).astype(jnp.bfloat16)
        returned = over_groups(produced.reshape(GROUPS, slots, width), first - 1).reshape(GROUPS * slots, width)
        added = jnp.dot(
            mix[step],
            returned.astype(jnp.float32),
            precision=lax.Precision.HIGHEST,
            preferred_element_type=jnp.float32,
        )
        result = (current.astype(jnp.float32) + added).astype(jnp.bfloat16)
        forward = shifted(result[:tokens], 1)
        backward = shifted(result[tokens:], -1)
        current = jnp.concatenate([forward, backward], axis=0)
    return current.reshape(1, streams, 1, tokens, width)


def solution(mesh):
    return jax.shard_map(
        shards,
        mesh=mesh,
        in_specs=(
            P("pipe", None, "expert", None, None),
            P("pipe", "expert", None, None),
            P("pipe", "expert", None, None),
            P("pipe", None),
            P(None, None, "pipe", None, None),
            P(None, None, "pipe", None, None),
        ),
        out_specs=P("pipe", None, "expert", None, None),
        check_vma=False,
    )
```
